32 devices in a mesh: tm: 4 (over x, core), range: 8 (over z, y).
Axes of the slice: x: 2, y: 2, z: 4, core: 2. Of those that a mesh axis runs over, the one named last changes fastest.
Arguments:
- slc_stack: bfloat16 [16, 2, 8192, 128], P('tm', None, 'range'), as said below
- pair_list: int32 [24, 2], P('tm'), may hold values from 0 to 15, as said below
Outputs:
- coherence_field: bfloat16 [24, 2, 8192, 128], P('tm', None, 'range')
The draws below stay inside these ranges and needn't reach their ends.
Inputs may be any that keep to these rules, and one draw needn't show every extreme that they name: `pair_list`: rows g * 6 to (g + 1) * 6 - 1 hold pairs whose reference (column 0) is one of the acquisitions g * 4 to (g + 1) * 4 - 1; the secondary (column 1) comes 1 to 3 acquisitions after the reference; no pair repeats. `slc_stack`: acquisitions of one scene with acquisition-dependent phase and noise.
All inputs are finite; a program needn't handle non-finite values.
Results may differ from the reference program's by a relative error of at most 0.001.
Values may be sent and summed in bfloat16 or wider, within the bound.
A program may use at most 64 MiB of HBM per device.

```python
import math
import jax
import jax.numpy as jnp
from jax import lax

ACQ_DEV = 4
LAG_MAX = 3
PAIR_DEV = 6
LINES = 128
LOOK_AZ = 5
LOOK_RG = 20
NACQ = 16
COLS = 8192


def draw_slc_stack(key, part):
    shape_all = (NACQ, 2, COLS, LINES)
    common = jax.random.normal(jax.random.fold_in(key, 11), (1, 2, COLS, LINES), jnp.float32)
    noise = jax.random.normal(jax.random.fold_in(key, 12), shape_all, jnp.float32)
    theta = 0.7 * jax.random.normal(jax.random.fold_in(key, 13), (NACQ, 1, COLS, LINES), jnp.float32)
    ratio = jnp.exp(jax.random.uniform(jax.random.fold_in(key, 14), (NACQ, 1, 1, 1), jnp.float32, math.log(0.3), math.log(3.0)))
    rot_real = jnp.cos(theta) * common[:, 0:1] - jnp.sin(theta) * common[:, 1:2]
    rot_imag = jnp.sin(theta) * common[:, 0:1] + jnp.cos(theta) * common[:, 1:2]
    rotated = jnp.concatenate([rot_real, rot_imag], axis=1)
    result = (rotated + ratio * noise) / jnp.sqrt(1.0 + ratio * ratio)
    return result.astype(jnp.bfloat16)


def draw_pair_list(key, part):
    groups = NACQ // ACQ_DEV
    candidates = ACQ_DEV * LAG_MAX
    cand_index = jnp.arange(candidates, dtype=jnp.int32)
    local_ref = cand_index // LAG_MAX
    lag_value = cand_index % LAG_MAX + 1

    def one_group(group):
        scores = jax.random.permutation(jax.random.fold_in(key, group + 100), candidates).astype(jnp.int32)
        global_ref = group * ACQ_DEV + local_ref
        valid = global_ref + lag_value < NACQ
        scores = jnp.where(valid, scores + candidates, -1 - cand_index)
        scores = jnp.where((group == 0) & (cand_index == 0), 3 * candidates, scores)
        chosen = lax.top_k(scores, PAIR_DEV)[1].astype(jnp.int32)
        ref_col = group * ACQ_DEV + chosen // LAG_MAX
        sec_col = ref_col + chosen % LAG_MAX + 1
        return jnp.stack([ref_col, sec_col], axis=1)
    rows = jax.vmap(one_group)(jnp.arange(groups, dtype=jnp.int32))
    return rows.reshape((groups * PAIR_DEV, 2)).astype(jnp.int32)


def setup_inputs(seed: int = 0) -> dict:
    arg_keys = jax.random.split(jax.random.key(seed), 3)
    return {
        "slc_stack": draw_slc_stack(jax.random.fold_in(arg_keys[2], 71), 0),
        "pair_list": draw_pair_list(jax.random.fold_in(arg_keys[2], 71), 0),
    }


EPSILON = 1e-06

def boxcar(values):
    lead_pad = [(0, 0)] * (values.ndim - 2)
    padded = jnp.pad(values, lead_pad + [(0, LOOK_RG - 1), (0, 0)])
    running = padded[..., 0:COLS, :]
    for j in range(1, LOOK_RG):
        running = running + padded[..., j:j + COLS, :]
    half_box = LOOK_AZ // 2
    padded = jnp.pad(running, lead_pad + [(0, 0), (half_box, LOOK_AZ - 1 - half_box)])
    summed = padded[..., 0:LINES]
    for j in range(1, LOOK_AZ):
        summed = summed + padded[..., j:j + LINES]
    return summed

def reference(slc_stack, pair_list):

    def power_of(acquisition):
        real_part = acquisition[0].astype(jnp.float32)
        imag_part = acquisition[1].astype(jnp.float32)
        return boxcar(real_part * real_part + imag_part * imag_part)
    powers_boxed = lax.map(power_of, slc_stack)

    def one_pair(pair_row):
        ref_acq = lax.dynamic_index_in_dim(slc_stack, pair_row[0], 0, keepdims=False).astype(jnp.float32)
        sec_acq = lax.dynamic_index_in_dim(slc_stack, pair_row[1], 0, keepdims=False).astype(jnp.float32)
        products = jnp.stack([ref_acq[0] * sec_acq[0] + ref_acq[1] * sec_acq[1], ref_acq[1] * sec_acq[0] - ref_acq[0] * sec_acq[1]])
        summed = boxcar(products)
        ref_power = lax.dynamic_index_in_dim(powers_boxed, pair_row[0], 0, keepdims=False)
        sec_power = lax.dynamic_index_in_dim(powers_boxed, pair_row[1], 0, keepdims=False)
        return (summed * lax.rsqrt(ref_power * sec_power + EPSILON)[None]).astype(jnp.bfloat16)
    return lax.map(one_pair, pair_list)
```

```python
import functools

import jax
import jax.numpy as jnp
from jax import lax
from jax.experimental import pallas as pl
from jax.experimental.pallas import tpu as pltpu
from jax.sharding import PartitionSpec as P

LAG_MAX = 3
LOOK_AZ = 5
LOOK_RG = 20
RIM = 32
CHUNK = 128
EPSILON = 1e-06
MESH = pl.DeviceIdType.MESH


def kernel(
    n_tm,
    n_range,
    pair_ref,
    slc_ref,
    out_ref,
    own,
    recv,
    work,
    field,
    twos,
    fours,
    boxed,
    own_sem,
    send_sem,
    recv_sem,
    rim_send,
    rim_recv,
):
    tm = lax.axis_index("tm")
    rg = lax.axis_index("range")
    acq_dev, _, cols, lines = slc_ref.shape
    n_pairs = out_ref.shape[0]
    n_chunks = cols // CHUNK
    n_acq = acq_dev + LAG_MAX
    has_next = tm < n_tm - 1
    has_prev = tm > 0
    has_right = rg < n_range - 1
    has_left = rg > 0

    def own_copy(c):
        at = pl.ds(pl.multiple_of(c * CHUNK, CHUNK), CHUNK)
        return pltpu.make_async_copy(slc_ref.at[:, :, at, :], own.at[:, :, at, :], own_sem.at[c])

    def chunk_copy(c):
        at = pl.ds(pl.multiple_of(c * CHUNK, CHUNK), CHUNK)
        return pltpu.make_async_remote_copy(
            src_ref=slc_ref.at[pl.ds(0, LAG_MAX), :, at, :],
            dst_ref=recv.at[:, :, at, :],
            send_sem=send_sem.at[c],
            recv_sem=recv_sem.at[c],
            device_id=(tm - 1, rg),
            device_id_type=MESH,
        )

    rim_copy = pltpu.make_async_remote_copy(
        src_ref=slc_ref.at[:, :, pl.ds(0, RIM), :],
        dst_ref=own.at[:, :, pl.ds(cols, RIM), :],
        send_sem=rim_send.at[0],
        recv_sem=rim_recv.at[0],
        device_id=(tm, rg - 1),
        device_id_type=MESH,
    )
    corner_copy = pltpu.make_async_remote_copy(
        src_ref=slc_ref.at[pl.ds(0, LAG_MAX), :, pl.ds(0, RIM), :],
        dst_ref=recv.at[:, :, pl.ds(cols, RIM), :],
        send_sem=rim_send.at[1],
        recv_sem=rim_recv.at[1],
        device_id=(tm - 1, rg - 1),
        device_id_type=MESH,
    )

    barrier = pltpu.get_barrier_semaphore()

    @pl.when(has_next)
    def _():
        pl.semaphore_signal(barrier, inc=1, device_id=(tm + 1, rg), device_id_type=MESH)

    @pl.when(has_right)
    def _():
        pl.semaphore_signal(barrier, inc=1, device_id=(tm, rg + 1), device_id_type=MESH)

    @pl.when(has_next & has_right)
    def _():
        pl.semaphore_signal(barrier, inc=1, device_id=(tm + 1, rg + 1), device_id_type=MESH)

    @pl.loop(0, n_chunks)
    def _(i):
        own_copy(n_chunks - 1 - i).start()

    prev_count = jnp.where(has_prev, 1, 0)
    left_count = jnp.where(has_left, 1, 0)

    @pl.when(has_prev | has_left)
    def _():
        pl.semaphore_wait(barrier, prev_count + left_count + prev_count * left_count)

    @pl.when(has_left)
    def _():
        rim_copy.start()

    @pl.when(has_prev & has_left)
    def _():
        corner_copy.start()

    @pl.when(has_prev)
    def _():
        @pl.loop(0, n_chunks)
        def _(i):
            chunk_copy(n_chunks - 1 - i).start()

    @pl.when(jnp.logical_not(has_next))
    def _():
        recv[...] = jnp.zeros_like(recv)

    @pl.when(has_next & jnp.logical_not(has_right))
    def _():
        recv[:, :, cols:, :] = jnp.zeros((LAG_MAX, 2, RIM, lines), recv.dtype)

    @pl.when(jnp.logical_not(has_right))
    def _():
        own[:, :, cols:, :] = jnp.zeros((acq_dev, 2, RIM, lines), own.dtype)

    @pl.when(has_right)
    def _():
        rim_copy.wait_recv()

    @pl.when(has_next & has_right)
    def _():
        corner_copy.wait_recv()

    half = LOOK_AZ // 2
    from_line = lax.rem(lax.broadcasted_iota(jnp.int32, (2 * lines, lines), 0), lines)
    to_line = lax.broadcasted_iota(jnp.int32, (2 * lines, lines), 1)
    near = (from_line - to_line >= -half) & (from_line - to_line <= LOOK_AZ - 1 - half)
    band = jnp.where(near, 1.0, 0.0).astype(jnp.bfloat16)
    first_acq = tm * acq_dev

    def box(k, value):
        field[k] = value
        twos[k] = field[k, 0 : CHUNK + 24, :] + field[k, 1 : CHUNK + 25, :]
        fours[k] = twos[k, 0 : CHUNK + 16, :] + twos[k, 2 : CHUNK + 18, :]
        running = fours[k, 0:CHUNK, :]
        for j in range(4, LOOK_RG, 4):
            running = running + fours[k, j : j + CHUNK, :]
        high = running.astype(jnp.bfloat16)
        low = (running - high.astype(jnp.float32)).astype(jnp.bfloat16)
        return jnp.dot(
            jnp.concatenate([high, low], axis=1), band, preferred_element_type=jnp.float32
        )

    @pl.loop(0, n_chunks)
    def _(i):
        c = n_chunks - 1 - i
        own_copy(c).wait()

        @pl.when(has_next)
        def _():
            chunk_copy(c).wait_recv()

        start = pl.multiple_of(c * CHUNK, CHUNK)
        at = pl.ds(start, CHUNK)
        ext = pl.ds(start, CHUNK + RIM)
        for k in range(n_acq):
            source = own.at[k] if k < acq_dev else recv.at[k - acq_dev]
            real = source[0, ext, :].astype(jnp.float32)
            imag = source[1, ext, :].astype(jnp.float32)
            work[k, 0] = real
            work[k, 1] = imag
            boxed[k] = box(k % 2, real * real + imag * imag)
        for p in range(n_pairs):
            ref = jnp.clip(pair_ref[0, p] - first_acq, 0, n_acq - 1)
            sec = jnp.clip(pair_ref[1, p] - first_acq, 0, n_acq - 1)
            r0, r1 = work[ref, 0], work[ref, 1]
            s0, s1 = work[sec, 0], work[sec, 1]
            norm = lax.rsqrt(boxed[ref] * boxed[sec] + EPSILON)
            out_ref[p, 0, at, :] = (box(0, r0 * s0 + r1 * s1) * norm).astype(out_ref.dtype)
            out_ref[p, 1, at, :] = (box(1, r1 * s0 - r0 * s1) * norm).astype(out_ref.dtype)

    @pl.when(has_left)
    def _():
        rim_copy.wait_send()

    @pl.when(has_prev & has_left)
    def _():
        corner_copy.wait_send()

    @pl.when(has_prev)
    def _():
        @pl.loop(0, n_chunks)
        def _(i):
            chunk_copy(n_chunks - 1 - i).wait_send()


def local(slc_stack, pair_list):
    acq_dev, _, cols, lines = slc_stack.shape
    n_pairs = pair_list.shape[0]
    n_acq = acq_dev + LAG_MAX
    n_chunks = cols // CHUNK
    f32 = jnp.float32
    return pl.pallas_call(
        functools.partial(kernel, lax.axis_size("tm"), lax.axis_size("range")),
        out_shape=jax.ShapeDtypeStruct((n_pairs, 2, cols, lines), jnp.bfloat16),
        in_specs=[
            pl.BlockSpec(memory_space=pltpu.SMEM),
            pl.BlockSpec(memory_space=pltpu.HBM),
        ],
        out_specs=pl.BlockSpec(memory_space=pltpu.VMEM),
        scratch_shapes=[
            pltpu.VMEM((acq_dev, 2, cols + RIM, lines), jnp.bfloat16),
            pltpu.VMEM((LAG_MAX, 2, cols + RIM, lines), jnp.bfloat16),
            pltpu.VMEM((n_acq, 2, CHUNK + RIM, lines), f32),
            pltpu.VMEM((2, CHUNK + RIM, lines), f32),
            pltpu.VMEM((2, CHUNK + 24, lines), f32),
            pltpu.VMEM((2, CHUNK + 16, lines), f32),
            pltpu.VMEM((n_acq, CHUNK, lines), f32),
            pltpu.SemaphoreType.DMA((n_chunks,)),
            pltpu.SemaphoreType.DMA((n_chunks,)),
            pltpu.SemaphoreType.DMA((n_chunks,)),
            pltpu.SemaphoreType.DMA((2,)),
            pltpu.SemaphoreType.DMA((2,)),
        ],
        compiler_params=pltpu.CompilerParams(
            collective_id=0, has_side_effects=True, vmem_limit_bytes=57 * 1024 * 1024
        ),
    )(pair_list.T, slc_stack)


def solution(mesh):
    in_specs = (P("tm", None, "range", None), P("tm", None))
    out_specs = P("tm", None, "range", None)
    return jax.shard_map(local, mesh=mesh, in_specs=in_specs, out_specs=out_specs, check_vma=False)
```

```python
import functools

import jax
import jax.numpy as jnp
from jax import lax
from jax.experimental import pallas as pl
from jax.experimental.pallas import tpu as pltpu
from jax.sharding import PartitionSpec as P

LAG_MAX = 3
LOOK_AZ = 5
LOOK_RG = 20
RIM = 32
CHUNK = 128
GROUP = 1
EPSILON = 1e-06
MESH = pl.DeviceIdType.MESH


def kernel(
    n_tm,
    n_range,
    pair_ref,
    slc_ref,
    out_ref,
    own,
    recv,
    work,
    field,
    twos,
    fours,
    boxed,
    own_sem,
    send_sem,
    recv_sem,
    rim_send,
    rim_recv,
):
    tm = lax.axis_index("tm")
    rg = lax.axis_index("range")
    acq_dev, _, cols, lines = slc_ref.shape
    n_pairs = out_ref.shape[0]
    n_chunks = cols // CHUNK
    n_acq = acq_dev + LAG_MAX
    has_next = tm < n_tm - 1
    has_prev = tm > 0
    has_right = rg < n_range - 1
    has_left = rg > 0

    def own_copy(c):
        at = pl.ds(pl.multiple_of(c * CHUNK, CHUNK), CHUNK)
        return pltpu.make_async_copy(slc_ref.at[:, :, at, :], own.at[:, :, at, :], own_sem.at[c])

    def chunk_copy(c):
        at = pl.ds(pl.multiple_of(c * CHUNK, CHUNK), CHUNK)
        return pltpu.make_async_remote_copy(
            src_ref=slc_ref.at[pl.ds(0, LAG_MAX), :, at, :],
            dst_ref=recv.at[:, :, at, :],
            send_sem=send_sem.at[c],
            recv_sem=recv_sem.at[c],
            device_id=(tm - 1, rg),
            device_id_type=MESH,
        )

    rim_copy = pltpu.make_async_remote_copy(
        src_ref=slc_ref.at[:, :, pl.ds(0, RIM), :],
        dst_ref=own.at[:, :, pl.ds(cols, RIM), :],
        send_sem=rim_send.at[0],
        recv_sem=rim_recv.at[0],
        device_id=(tm, rg - 1),
        device_id_type=MESH,
    )
    corner_copy = pltpu.make_async_remote_copy(
        src_ref=slc_ref.at[pl.ds(0, LAG_MAX), :, pl.ds(0, RIM), :],
        dst_ref=recv.at[:, :, pl.ds(cols, RIM), :],
        send_sem=rim_send.at[1],
        recv_sem=rim_recv.at[1],
        device_id=(tm - 1, rg - 1),
        device_id_type=MESH,
    )

    barrier = pltpu.get_barrier_semaphore()

    @pl.when(has_next)
    def _():
        pl.semaphore_signal(barrier, inc=1, device_id=(tm + 1, rg), device_id_type=MESH)

    @pl.when(has_right)
    def _():
        pl.semaphore_signal(barrier, inc=1, device_id=(tm, rg + 1), device_id_type=MESH)

    @pl.when(has_next & has_right)
    def _():
        pl.semaphore_signal(barrier, inc=1, device_id=(tm + 1, rg + 1), device_id_type=MESH)

    @pl.loop(0, n_chunks)
    def _(i):
        own_copy(n_chunks - 1 - i).start()

    prev_count = jnp.where(has_prev, 1, 0)
    left_count = jnp.where(has_left, 1, 0)

    @pl.when(has_prev | has_left)
    def _():
        pl.semaphore_wait(barrier, prev_count + left_count + prev_count * left_count)

    @pl.when(has_left)
    def _():
        rim_copy.start()

    @pl.when(has_prev & has_left)
    def _():
        corner_copy.start()

    @pl.when(has_prev)
    def _():
        @pl.loop(0, n_chunks)
        def _(i):
            chunk_copy(n_chunks - 1 - i).start()

    @pl.when(jnp.logical_not(has_next))
    def _():
        recv[...] = jnp.zeros_like(recv)

    @pl.when(has_next & jnp.logical_not(has_right))
    def _():
        recv[:, :, cols:, :] = jnp.zeros((LAG_MAX, 2, RIM, lines), recv.dtype)

    @pl.when(jnp.logical_not(has_right))
    def _():
        own[:, :, cols:, :] = jnp.zeros((acq_dev, 2, RIM, lines), own.dtype)

    @pl.when(has_right)
    def _():
        rim_copy.wait_recv()

    @pl.when(has_next & has_right)
    def _():
        corner_copy.wait_recv()

    half = LOOK_AZ // 2
    from_line = lax.rem(lax.broadcasted_iota(jnp.int32, (2 * lines, lines), 0), lines)
    to_line = lax.broadcasted_iota(jnp.int32, (2 * lines, lines), 1)
    near = (from_line - to_line >= -half) & (from_line - to_line <= LOOK_AZ - 1 - half)
    band = jnp.where(near, 1.0, 0.0).astype(jnp.bfloat16)
    first_acq = tm * acq_dev

    def box(slot, values):
        parts = []
        for k, value in enumerate(values, slot):
            field[k] = value
        for k in range(slot, slot + len(values)):
            twos[k] = field[k, 0 : CHUNK + 24, :] + field[k, 1 : CHUNK + 25, :]
        for k in range(slot, slot + len(values)):
            fours[k] = twos[k, 0 : CHUNK + 16, :] + twos[k, 2 : CHUNK + 18, :]
        for k in range(slot, slot + len(values)):
            running = fours[k, 0:CHUNK, :]
            for j in range(4, LOOK_RG, 4):
                running = running + fours[k, j : j + CHUNK, :]
            high = running.astype(jnp.bfloat16)
            low = (running - high.astype(jnp.float32)).astype(jnp.bfloat16)
            parts.append(jnp.concatenate([high, low], axis=1))
        summed = jnp.dot(
            jnp.concatenate(parts, axis=0), band, preferred_element_type=jnp.float32
        )
        return [summed[k * CHUNK : (k + 1) * CHUNK] for k in range(len(values))]

    @pl.loop(0, n_chunks)
    def _(i):
        c = n_chunks - 1 - i
        own_copy(c).wait()

        @pl.when(has_next)
        def _():
            chunk_copy(c).wait_recv()

        start = pl.multiple_of(c * CHUNK, CHUNK)
        at = pl.ds(start, CHUNK)
        ext = pl.ds(start, CHUNK + RIM)
        powers = []
        for k in range(n_acq):
            source = own.at[k] if k < acq_dev else recv.at[k - acq_dev]
            real = source[0, ext, :].astype(jnp.float32)
            imag = source[1, ext, :].astype(jnp.float32)
            work[k, 0] = real
            work[k, 1] = imag
            powers.append(real * real + imag * imag)
        for k, value in enumerate(box(0, powers)):
            boxed[k] = value
        slot = n_acq
        for first in range(0, n_pairs, GROUP):
            group = range(first, min(first + GROUP, n_pairs))
            products, norms = [], []
            for p in group:
                ref = jnp.clip(pair_ref[0, p] - first_acq, 0, n_acq - 1)
                sec = jnp.clip(pair_ref[1, p] - first_acq, 0, n_acq - 1)
                r0, r1 = work[ref, 0], work[ref, 1]
                s0, s1 = work[sec, 0], work[sec, 1]
                products += [r0 * s0 + r1 * s1, r1 * s0 - r0 * s1]
                norms.append(lax.rsqrt(boxed[ref] * boxed[sec] + EPSILON))
            summed = box(slot, products)
            slot += len(products)
            for q, p in enumerate(group):
                out_ref[p, 0, at, :] = (summed[2 * q] * norms[q]).astype(out_ref.dtype)
                out_ref[p, 1, at, :] = (summed[2 * q + 1] * norms[q]).astype(out_ref.dtype)

    @pl.when(has_left)
    def _():
        rim_copy.wait_send()

    @pl.when(has_prev & has_left)
    def _():
        corner_copy.wait_send()

    @pl.when(has_prev)
    def _():
        @pl.loop(0, n_chunks)
        def _(i):
            chunk_copy(n_chunks - 1 - i).wait_send()


def local(slc_stack, pair_list):
    acq_dev, _, cols, lines = slc_stack.shape
    n_pairs = pair_list.shape[0]
    n_acq = acq_dev + LAG_MAX
    n_chunks = cols // CHUNK
    n_fields = n_acq + 2 * n_pairs
    f32 = jnp.float32
    return pl.pallas_call(
        functools.partial(kernel, lax.axis_size("tm"), lax.axis_size("range")),
        out_shape=jax.ShapeDtypeStruct((n_pairs, 2, cols, lines), jnp.bfloat16),
        in_specs=[
            pl.BlockSpec(memory_space=pltpu.SMEM),
            pl.BlockSpec(memory_space=pltpu.HBM),
        ],
        out_specs=pl.BlockSpec(memory_space=pltpu.VMEM),
        scratch_shapes=[
            pltpu.VMEM((acq_dev, 2, cols + RIM, lines), jnp.bfloat16),
            pltpu.VMEM((LAG_MAX, 2, cols + RIM, lines), jnp.bfloat16),
            pltpu.VMEM((n_acq, 2, CHUNK + RIM, lines), f32),
            pltpu.VMEM((n_fields, CHUNK + RIM, lines), f32),
            pltpu.VMEM((n_fields, CHUNK + 24, lines), f32),
            pltpu.VMEM((n_fields, CHUNK + 16, lines), f32),
            pltpu.VMEM((n_acq, CHUNK, lines), f32),
            pltpu.SemaphoreType.DMA((n_chunks,)),
            pltpu.SemaphoreType.DMA((n_chunks,)),
            pltpu.SemaphoreType.DMA((n_chunks,)),
            pltpu.SemaphoreType.DMA((2,)),
            pltpu.SemaphoreType.DMA((2,)),
        ],
        compiler_params=pltpu.CompilerParams(
            collective_id=0, has_side_effects=True, vmem_limit_bytes=32 * 1024 * 1024
        ),
    )(
        pltpu.with_memory_space_constraint(pair_list.T, pltpu.HBM),
        pltpu.with_memory_space_constraint(slc_stack, pltpu.HBM),
    )


def solution(mesh):
    in_specs = (P("tm", None, "range", None), P("tm", None))
    out_specs = P("tm", None, "range", None)
    return jax.shard_map(local, mesh=mesh, in_specs=in_specs, out_specs=out_specs, check_vma=False)
```

```python
import functools

import jax
import jax.numpy as jnp
from jax import lax
from jax.experimental import pallas as pl
from jax.experimental.pallas import tpu as pltpu
from jax.sharding import PartitionSpec as P

LAG_MAX = 3
LOOK_AZ = 5
LOOK_RG = 20
RIM = 32
CHUNK = 128
EPSILON = 1e-06
MESH = pl.DeviceIdType.MESH


def band_matrix(lines):
    half = LOOK_AZ // 2
    from_line = lax.rem(lax.broadcasted_iota(jnp.int32, (2 * lines, lines), 0), lines)
    to_line = lax.broadcasted_iota(jnp.int32, (2 * lines, lines), 1)
    near = (from_line - to_line >= -half) & (from_line - to_line <= LOOK_AZ - 1 - half)
    return jnp.where(near, 1.0, 0.0).astype(jnp.bfloat16)


def box(slot, values, band, field, twos, fours):
    parts = []
    slots = range(slot, slot + len(values))
    for k, value in zip(slots, values):
        field[k] = value
    for k in slots:
        twos[k] = field[k, 0 : CHUNK + 24, :] + field[k, 1 : CHUNK + 25, :]
    for k in slots:
        fours[k] = twos[k, 0 : CHUNK + 16, :] + twos[k, 2 : CHUNK + 18, :]
    for k in slots:
        running = fours[k, 0:CHUNK, :]
        for j in range(4, LOOK_RG, 4):
            running = running + fours[k, j : j + CHUNK, :]
        high = running.astype(jnp.bfloat16)
        low = (running - high.astype(jnp.float32)).astype(jnp.bfloat16)
        parts.append(jnp.concatenate([high, low], axis=1))
    summed = jnp.dot(jnp.concatenate(parts, axis=0), band, preferred_element_type=jnp.float32)
    return [summed[k * CHUNK : (k + 1) * CHUNK] for k in range(len(values))]


def coherence(pair_ref, first_acq, work, boxed, band, field, twos, fours, emit):
    n_acq = work.shape[0]
    n_pairs = pair_ref.shape[1]
    powers = [work[k, 0] * work[k, 0] + work[k, 1] * work[k, 1] for k in range(n_acq)]
    for k, value in enumerate(box(0, powers, band, field, twos, fours)):
        boxed[k] = value
    slot = n_acq
    for p in range(n_pairs):
        ref = jnp.clip(pair_ref[0, p] - first_acq, 0, n_acq - 1)
        sec = jnp.clip(pair_ref[1, p] - first_acq, 0, n_acq - 1)
        r0, r1 = work[ref, 0], work[ref, 1]
        s0, s1 = work[sec, 0], work[sec, 1]
        norm = lax.rsqrt(boxed[ref] * boxed[sec] + EPSILON)
        products = [r0 * s0 + r1 * s1, r1 * s0 - r0 * s1]
        real, imag = box(slot, products, band, field, twos, fours)
        slot += 2
        emit(p, (real * norm).astype(jnp.bfloat16), (imag * norm).astype(jnp.bfloat16))


def kernel(
    n_tm,
    n_range,
    pair_ref,
    slc_ref,
    out_ref,
    last_ref,
    own,
    recv,
    work,
    field,
    twos,
    fours,
    boxed,
    own_sem,
    send_sem,
    recv_sem,
    rim_send,
    rim_recv,
):
    tm = lax.axis_index("tm")
    rg = lax.axis_index("range")
    acq_dev, _, cols, lines = slc_ref.shape
    n_chunks = cols // CHUNK
    n_acq = acq_dev + LAG_MAX
    has_next = tm < n_tm - 1
    has_prev = tm > 0
    has_right = rg < n_range - 1
    has_left = rg > 0

    own_copy = pltpu.make_async_copy(slc_ref, own.at[:, :, pl.ds(0, cols), :], own_sem)

    def piece_copy(k, at):
        return pltpu.make_async_remote_copy(
            src_ref=slc_ref.at[pl.ds(0, LAG_MAX), :, at, :],
            dst_ref=recv.at[:, :, at, :],
            send_sem=send_sem.at[k],
            recv_sem=recv_sem.at[k],
            device_id=(tm - 1, rg),
            device_id_type=MESH,
        )

    def middle_piece(k):
        return piece_copy(k, pl.ds(pl.multiple_of(k * CHUNK + RIM, RIM), CHUNK))

    first_piece = piece_copy(0, pl.ds(0, CHUNK + RIM))
    last_piece = piece_copy(n_chunks - 1, pl.ds(cols - CHUNK + RIM, CHUNK - RIM))
    rim_copy = pltpu.make_async_remote_copy(
        src_ref=slc_ref.at[:, :, pl.ds(0, RIM), :],
        dst_ref=own.at[:, :, pl.ds(cols, RIM), :],
        send_sem=rim_send.at[0],
        recv_sem=rim_recv.at[0],
        device_id=(tm, rg - 1),
        device_id_type=MESH,
    )
    corner_copy = pltpu.make_async_remote_copy(
        src_ref=recv.at[:, :, pl.ds(0, RIM), :],
        dst_ref=recv.at[:, :, pl.ds(cols, RIM), :],
        send_sem=rim_send.at[1],
        recv_sem=rim_recv.at[1],
        device_id=(tm, rg - 1),
        device_id_type=MESH,
    )

    barrier = pltpu.get_barrier_semaphore()

    @pl.when(has_next)
    def _():
        pl.semaphore_signal(barrier, inc=1, device_id=(tm + 1, rg), device_id_type=MESH)

    @pl.when(has_right)
    def _():
        pl.semaphore_signal(barrier, inc=1, device_id=(tm, rg + 1), device_id_type=MESH)

    own_copy.start()

    @pl.when(has_prev | has_left)
    def _():
        pl.semaphore_wait(barrier, jnp.where(has_prev, 1, 0) + jnp.where(has_left, 1, 0))

    @pl.when(has_prev)
    def _():
        first_piece.start()

    @pl.when(has_left)
    def _():
        rim_copy.start()

    @pl.when(has_prev)
    def _():
        @pl.loop(1, n_chunks - 1)
        def _(k):
            middle_piece(k).start()

        last_piece.start()

    @pl.when(jnp.logical_not(has_next))
    def _():
        recv[...] = jnp.zeros_like(recv)

    @pl.when(has_next & jnp.logical_not(has_right))
    def _():
        recv[:, :, cols:, :] = jnp.zeros((LAG_MAX, 2, RIM, lines), recv.dtype)

    @pl.when(jnp.logical_not(has_right))
    def _():
        own[:, :, cols:, :] = jnp.zeros((acq_dev, 2, RIM, lines), own.dtype)

    band = band_matrix(lines)
    own_copy.wait()

    def gather(target, start):
        ext = pl.ds(start, CHUNK + RIM)
        for k in range(n_acq):
            source = own.at[k] if k < acq_dev else recv.at[k - acq_dev]
            target[k, 0] = source[0, ext, :].astype(jnp.float32)
            target[k, 1] = source[1, ext, :].astype(jnp.float32)

    @pl.when(has_next)
    def _():
        first_piece.wait_recv()

    @pl.when(has_next & has_left)
    def _():
        corner_copy.start()

    @pl.loop(0, n_chunks - 1)
    def _(c):
        @pl.when(has_next & (c > 0))
        def _():
            middle_piece(c).wait_recv()

        start = pl.multiple_of(c * CHUNK, CHUNK)
        gather(work, start)

        def emit(p, real, imag):
            out_ref[p, 0, pl.ds(start, CHUNK), :] = real
            out_ref[p, 1, pl.ds(start, CHUNK), :] = imag

        coherence(pair_ref, tm * acq_dev, work, boxed, band, field, twos, fours, emit)

    @pl.when(has_right)
    def _():
        rim_copy.wait_recv()

    @pl.when(has_next & has_right)
    def _():
        corner_copy.wait_recv()

    @pl.when(has_next)
    def _():
        last_piece.wait_recv()

    gather(last_ref, cols - CHUNK)

    @pl.when(has_left)
    def _():
        rim_copy.wait_send()

    @pl.when(has_next & has_left)
    def _():
        corner_copy.wait_send()

    @pl.when(has_prev)
    def _():
        first_piece.wait_send()

        @pl.loop(1, n_chunks - 1)
        def _(k):
            middle_piece(k).wait_send()

        last_piece.wait_send()


def finish(pair_ref, done_ref, work, out_ref, last, field, twos, fours, boxed, done_sem, last_sem):
    n_pairs, _, cols, lines = out_ref.shape
    n_acq = work.shape[0]
    before = pl.ds(0, cols - CHUNK)
    after = pl.ds(cols - CHUNK, CHUNK)
    early = [
        pltpu.make_async_copy(done_ref.at[p, :, before], out_ref.at[p, :, before], done_sem.at[p])
        for p in range(n_pairs)
    ]
    late = [
        pltpu.make_async_copy(last.at[p], out_ref.at[p, :, after], last_sem.at[p])
        for p in range(n_pairs)
    ]
    for copy in early:
        copy.start()

    def emit(p, real, imag):
        last[p, 0] = real
        last[p, 1] = imag
        late[p].start()

    first_acq = lax.axis_index("tm") * (n_acq - LAG_MAX)
    coherence(
        pair_ref, first_acq, work, boxed, band_matrix(lines), field, twos, fours, emit
    )
    for copy in early + late:
        copy.wait()


def local(slc_stack, pair_list):
    acq_dev, _, cols, lines = slc_stack.shape
    n_pairs = pair_list.shape[0]
    n_acq = acq_dev + LAG_MAX
    n_chunks = cols // CHUNK
    n_fields = n_acq + 2 * n_pairs
    f32, bf16 = jnp.float32, jnp.bfloat16
    box_scratch = [
        pltpu.VMEM((n_fields, CHUNK + RIM, lines), f32),
        pltpu.VMEM((n_fields, CHUNK + 24, lines), f32),
        pltpu.VMEM((n_fields, CHUNK + 16, lines), f32),
        pltpu.VMEM((n_acq, CHUNK, lines), f32),
    ]
    smem = pl.BlockSpec(memory_space=pltpu.SMEM)
    vmem = pl.BlockSpec(memory_space=pltpu.VMEM)
    hbm = pl.BlockSpec(memory_space=pltpu.HBM)
    pairs = pltpu.with_memory_space_constraint(pair_list.T, pltpu.HBM)
    done, last = pl.pallas_call(
        functools.partial(kernel, lax.axis_size("tm"), lax.axis_size("range")),
        out_shape=(
            pltpu.VMEM((n_pairs, 2, cols, lines), bf16),
            pltpu.VMEM((n_acq, 2, CHUNK + RIM, lines), f32),
        ),
        in_specs=[smem, hbm],
        out_specs=(vmem, vmem),
        scratch_shapes=[
            pltpu.VMEM((acq_dev, 2, cols + RIM, lines), bf16),
            pltpu.VMEM((LAG_MAX, 2, cols + RIM, lines), bf16),
            pltpu.VMEM((n_acq, 2, CHUNK + RIM, lines), f32),
            *box_scratch,
            pltpu.SemaphoreType.DMA,
            pltpu.SemaphoreType.DMA((n_chunks,)),
            pltpu.SemaphoreType.DMA((n_chunks,)),
            pltpu.SemaphoreType.DMA((2,)),
            pltpu.SemaphoreType.DMA((2,)),
        ],
        compiler_params=pltpu.CompilerParams(
            collective_id=0, has_side_effects=True, vmem_limit_bytes=32 * 1024 * 1024
        ),
    )(pairs, pltpu.with_memory_space_constraint(slc_stack, pltpu.HBM))
    return pl.pallas_call(
        finish,
        out_shape=jax.ShapeDtypeStruct((n_pairs, 2, cols, lines), bf16),
        in_specs=[smem, vmem, vmem],
        out_specs=hbm,
        scratch_shapes=[
            pltpu.VMEM((n_pairs, 2, CHUNK, lines), bf16),
            *box_scratch,
            pltpu.SemaphoreType.DMA((n_pairs,)),
            pltpu.SemaphoreType.DMA((n_pairs,)),
        ],
        compiler_params=pltpu.CompilerParams(vmem_limit_bytes=32 * 1024 * 1024),
    )(pair_list.T, done, last)


def solution(mesh):
    in_specs = (P("tm", None, "range", None), P("tm", None))
    out_specs = P("tm", None, "range", None)
    return jax.shard_map(local, mesh=mesh, in_specs=in_specs, out_specs=out_specs, check_vma=False)
```

```python
import functools

import jax
import jax.numpy as jnp
from jax import lax
from jax.experimental import pallas as pl
from jax.experimental.pallas import tpu as pltpu
from jax.sharding import PartitionSpec as P

LAG_MAX = 3
LOOK_AZ = 5
LOOK_RG = 20
RIM = 32
CHUNK = 128
EPSILON = 1e-06
MESH = pl.DeviceIdType.MESH


def band_matrix(lines):
    half = LOOK_AZ // 2
    from_line = lax.rem(lax.broadcasted_iota(jnp.int32, (2 * lines, lines), 0), lines)
    to_line = lax.broadcasted_iota(jnp.int32, (2 * lines, lines), 1)
    near = (from_line - to_line >= -half) & (from_line - to_line <= LOOK_AZ - 1 - half)
    return jnp.where(near, 1.0, 0.0).astype(jnp.bfloat16)


def box(slot, values, band, field, twos, fours):
    parts = []
    slots = range(slot, slot + len(values))
    for k, value in zip(slots, values):
        field[k] = value
    for k in slots:
        twos[k] = field[k, 0 : CHUNK + 24, :] + field[k, 1 : CHUNK + 25, :]
    for k in slots:
        fours[k] = twos[k, 0 : CHUNK + 16, :] + twos[k, 2 : CHUNK + 18, :]
    for k in slots:
        running = fours[k, 0:CHUNK, :]
        for j in range(4, LOOK_RG, 4):
            running = running + fours[k, j : j + CHUNK, :]
        high = running.astype(jnp.bfloat16)
        low = (running - high.astype(jnp.float32)).astype(jnp.bfloat16)
        parts.append(jnp.concatenate([high, low], axis=1))
    summed = jnp.dot(jnp.concatenate(parts, axis=0), band, preferred_element_type=jnp.float32)
    return [summed[k * CHUNK : (k + 1) * CHUNK] for k in range(len(values))]


def coherence(pair_ref, first_acq, work, boxed, band, field, twos, fours, emit):
    n_acq = work.shape[0]
    n_pairs = pair_ref.shape[1]
    powers = [work[k, 0] * work[k, 0] + work[k, 1] * work[k, 1] for k in range(n_acq)]
    for k, value in enumerate(box(0, powers, band, field, twos, fours)):
        boxed[k] = value
    slot = n_acq
    for p in range(n_pairs):
        ref = jnp.clip(pair_ref[0, p] - first_acq, 0, n_acq - 1)
        sec = jnp.clip(pair_ref[1, p] - first_acq, 0, n_acq - 1)
        r0, r1 = work[ref, 0], work[ref, 1]
        s0, s1 = work[sec, 0], work[sec, 1]
        norm = lax.rsqrt(boxed[ref] * boxed[sec] + EPSILON)
        products = [r0 * s0 + r1 * s1, r1 * s0 - r0 * s1]
        real, imag = box(slot, products, band, field, twos, fours)
        slot += 2
        emit(p, (real * norm).astype(jnp.bfloat16), (imag * norm).astype(jnp.bfloat16))


def kernel(
    n_tm,
    n_range,
    pair_ref,
    slc_ref,
    out_ref,
    own,
    recv,
    work,
    field,
    twos,
    fours,
    boxed,
    own_sem,
    send_sem,
    recv_sem,
    rim_send,
    rim_recv,
):
    tm = lax.axis_index("tm")
    rg = lax.axis_index("range")
    acq_dev, _, cols, lines = slc_ref.shape
    n_chunks = cols // CHUNK
    n_acq = acq_dev + LAG_MAX
    has_next = tm < n_tm - 1
    has_prev = tm > 0
    has_right = rg < n_range - 1
    has_left = rg > 0

    own_copy = pltpu.make_async_copy(slc_ref, own.at[:, :, pl.ds(0, cols), :], own_sem)

    def piece_copy(k, at):
        return pltpu.make_async_remote_copy(
            src_ref=slc_ref.at[pl.ds(0, LAG_MAX), :, at, :],
            dst_ref=recv.at[:, :, at, :],
            send_sem=send_sem.at[k],
            recv_sem=recv_sem.at[k],
            device_id=(tm - 1, rg),
            device_id_type=MESH,
        )

    def middle_piece(k):
        return piece_copy(k, pl.ds(pl.multiple_of(k * CHUNK + RIM, RIM), CHUNK))

    first_piece = piece_copy(0, pl.ds(0, CHUNK + RIM))
    last_piece = piece_copy(n_chunks - 1, pl.ds(cols - CHUNK + RIM, CHUNK - RIM))
    rim_copy = pltpu.make_async_remote_copy(
        src_ref=slc_ref.at[:, :, pl.ds(0, RIM), :],
        dst_ref=own.at[:, :, pl.ds(cols, RIM), :],
        send_sem=rim_send.at[0],
        recv_sem=rim_recv.at[0],
        device_id=(tm, rg - 1),
        device_id_type=MESH,
    )
    corner_copy = pltpu.make_async_remote_copy(
        src_ref=recv.at[:, :, pl.ds(0, RIM), :],
        dst_ref=recv.at[:, :, pl.ds(cols, RIM), :],
        send_sem=rim_send.at[1],
        recv_sem=rim_recv.at[1],
        device_id=(tm, rg - 1),
        device_id_type=MESH,
    )

    barrier = pltpu.get_barrier_semaphore()

    @pl.when(has_next)
    def _():
        pl.semaphore_signal(barrier, inc=1, device_id=(tm + 1, rg), device_id_type=MESH)

    @pl.when(has_right)
    def _():
        pl.semaphore_signal(barrier, inc=1, device_id=(tm, rg + 1), device_id_type=MESH)

    own_copy.start()

    @pl.when(has_prev | has_left)
    def _():
        pl.semaphore_wait(barrier, jnp.where(has_prev, 1, 0) + jnp.where(has_left, 1, 0))

    @pl.when(has_prev)
    def _():
        first_piece.start()

    @pl.when(has_left)
    def _():
        rim_copy.start()

    @pl.when(has_prev)
    def _():
        @pl.loop(1, n_chunks - 1)
        def _(k):
            middle_piece(k).start()

        last_piece.start()

    @pl.when(jnp.logical_not(has_next))
    def _():
        recv[...] = jnp.zeros_like(recv)

    @pl.when(has_next & jnp.logical_not(has_right))
    def _():
        recv[:, :, cols:, :] = jnp.zeros((LAG_MAX, 2, RIM, lines), recv.dtype)

    @pl.when(jnp.logical_not(has_right))
    def _():
        own[:, :, cols:, :] = jnp.zeros((acq_dev, 2, RIM, lines), own.dtype)

    band = band_matrix(lines)
    own_copy.wait()

    def gather(target, start):
        ext = pl.ds(start, CHUNK + RIM)
        for k in range(n_acq):
            source = own.at[k] if k < acq_dev else recv.at[k - acq_dev]
            target[k, 0] = source[0, ext, :].astype(jnp.float32)
            target[k, 1] = source[1, ext, :].astype(jnp.float32)

    def chunk(start):
        gather(work, start)

        def emit(p, real, imag):
            out_ref[p, 0, pl.ds(start, CHUNK), :] = real
            out_ref[p, 1, pl.ds(start, CHUNK), :] = imag

        coherence(pair_ref, tm * acq_dev, work, boxed, band, field, twos, fours, emit)

    @pl.when(has_next)
    def _():
        first_piece.wait_recv()

    @pl.when(has_next & has_left)
    def _():
        corner_copy.start()

    @pl.loop(0, n_chunks - 1)
    def _(c):
        @pl.when(has_next & (c > 0))
        def _():
            middle_piece(c).wait_recv()

        chunk(pl.multiple_of(c * CHUNK, CHUNK))

    @pl.when(has_right)
    def _():
        rim_copy.wait_recv()

    @pl.when(has_next & has_right)
    def _():
        corner_copy.wait_recv()

    @pl.when(has_next)
    def _():
        last_piece.wait_recv()

    chunk(cols - CHUNK)

    @pl.when(has_left)
    def _():
        rim_copy.wait_send()

    @pl.when(has_next & has_left)
    def _():
        corner_copy.wait_send()

    @pl.when(has_prev)
    def _():
        first_piece.wait_send()

        @pl.loop(1, n_chunks - 1)
        def _(k):
            middle_piece(k).wait_send()

        last_piece.wait_send()


def local(slc_stack, pair_list):
    acq_dev, _, cols, lines = slc_stack.shape
    n_pairs = pair_list.shape[0]
    n_acq = acq_dev + LAG_MAX
    n_chunks = cols // CHUNK
    n_fields = n_acq + 2 * n_pairs
    f32, bf16 = jnp.float32, jnp.bfloat16
    box_scratch = [
        pltpu.VMEM((n_fields, CHUNK + RIM, lines), f32),
        pltpu.VMEM((n_fields, CHUNK + 24, lines), f32),
        pltpu.VMEM((n_fields, CHUNK + 16, lines), f32),
        pltpu.VMEM((n_acq, CHUNK, lines), f32),
    ]
    smem = pl.BlockSpec(memory_space=pltpu.SMEM)
    vmem = pl.BlockSpec(memory_space=pltpu.VMEM)
    hbm = pl.BlockSpec(memory_space=pltpu.HBM)
    pairs = pltpu.with_memory_space_constraint(pair_list.T, pltpu.HBM)
    return pl.pallas_call(
        functools.partial(kernel, lax.axis_size("tm"), lax.axis_size("range")),
        out_shape=pltpu.VMEM((n_pairs, 2, cols, lines), bf16),
        in_specs=[smem, hbm],
        out_specs=vmem,
        scratch_shapes=[
            pltpu.VMEM((acq_dev, 2, cols + RIM, lines), bf16),
            pltpu.VMEM((LAG_MAX, 2, cols + RIM, lines), bf16),
            pltpu.VMEM((n_acq, 2, CHUNK + RIM, lines), f32),
            *box_scratch,
            pltpu.SemaphoreType.DMA,
            pltpu.SemaphoreType.DMA((n_chunks,)),
            pltpu.SemaphoreType.DMA((n_chunks,)),
            pltpu.SemaphoreType.DMA((2,)),
            pltpu.SemaphoreType.DMA((2,)),
        ],
        compiler_params=pltpu.CompilerParams(
            collective_id=0, has_side_effects=True, vmem_limit_bytes=32 * 1024 * 1024
        ),
    )(pairs, pltpu.with_memory_space_constraint(slc_stack, pltpu.HBM))


def solution(mesh):
    in_specs = (P("tm", None, "range", None), P("tm", None))
    out_specs = P("tm", None, "range", None)
    return jax.shard_map(local, mesh=mesh, in_specs=in_specs, out_specs=out_specs, check_vma=False)
```
